128 devices in a mesh: gx: 16 (over y, z_hi, core), gy: 8 (over x, z_lo).
Axes of the slice: x: 4, y: 4, z: 4 (z_hi: 2, z_lo: 2; z = z_hi * 2 + z_lo), core: 2. Of those that a mesh axis runs over, the one named last changes fastest.
Arguments:
- lam_start: float32 [64, 32, 1024], P(None, 'gx', 'gy'), may hold values from -6 to 6
- adj_rhs: float32 [64, 32, 1024], P(None, 'gx', 'gy'), may hold values from -6 to 6
- a_diag: bfloat16 [64, 64, 32, 1024], P(None, None, 'gx', 'gy')
- a_off: bfloat16 [4, 64, 64, 32, 1024], P(None, None, None, 'gx', 'gy'), may hold values from -0.119628906 to 0.119628906
- cols: int32 [4, 32, 1024], P(None, 'gx', 'gy'), may hold values from -1 to 32767, as said below
- smoother: bfloat16 [64, 64, 32, 1024], P(None, None, 'gx', 'gy')
- forward_u: float32 [64, 32, 1024], P(None, 'gx', 'gy'), may hold values from -6 to 6
- density: float32 [64, 32, 1024], P(None, 'gx', 'gy'), may hold values from 0.3 to 1
- owner_dev: int32 [16, 8, 256, 16], P('gx', 'gy'), may hold values from 0 to 127, all different within a row; in each aligned block of 256 rows (0 to 255, 256 to 511, ..., all dimensions but the last counted through in order) at most 64 rows name the same one
- owner_slot: int32 [16, 8, 256, 16], P('gx', 'gy'), may hold values from 0 to 255
- filt_weight: float32 [16, 8, 256, 16], P('gx', 'gy'), may hold values from 0.2 to 1
Outputs:
- adjoint: float32 [64, 32, 1024], P(None, 'gx', 'gy')
- filtered: float32 [64, 32, 1024], P(None, 'gx', 'gy')
The draws below stay inside these ranges and needn't reach their ends.
Inputs may be any that keep to these rules, and one draw needn't show every extreme that they name: `cols`: for each block (x, y) the four entries are the indices x' * 1024 + y' of its four face neighbours (x +- 1, y), (x, y +- 1) in an order that varies from block to block, -1 for a neighbour beyond the grid's edge. `owner_dev`: each element block names 16 different ranks; the 256 element blocks of one device name any rank at most 64 times, a bound that some block reaches.
All inputs are finite; a program needn't handle non-finite values.
Results may differ from the reference program's by a relative error of at most 0.0003.
Values sent between devices are 32-bit elements; how exact they have to be, the bound alone decides.
A program may use at most 128 MiB of HBM per device.

```python
import math
import jax
import jax.numpy as jnp
import numpy as np
from jax import lax

P_SIZE = 64
SWEEPS = 3
R = 16
BX = 2
BY = 128
NB = 256
GX = 32
GY = 1024
CAP = 64
N_GX = 16
N_GY = 8
DEVICES = 128


def draw_a_diag(key, part):
    key = jax.random.fold_in(key, 3)
    identity = jnp.eye(P_SIZE, dtype=jnp.float32)[:, :, None, None]
    jitter = 0.02 * jax.random.normal(key, (P_SIZE, P_SIZE, GX, GY), jnp.float32)
    return (identity + jitter).astype(jnp.bfloat16)


def draw_smoother(key, part):
    key = jax.random.fold_in(key, 5)
    identity = jnp.eye(P_SIZE, dtype=jnp.float32)[:, :, None, None]
    jitter = 0.015 * jax.random.normal(key, (P_SIZE, P_SIZE, GX, GY), jnp.float32)
    return (0.9 * identity + jitter).astype(jnp.bfloat16)


def draw_cols(key, part):
    key = jax.random.fold_in(key, 7)
    x_index = jnp.arange(GX, dtype=jnp.int32)[:, None]
    y_index = jnp.arange(GY, dtype=jnp.int32)[None, :]
    neighbour_ids = jnp.stack([jnp.where(x_index >= 1, (x_index - 1) * GY + y_index, -1), jnp.where(x_index < GX - 1, (x_index + 1) * GY + y_index, -1), jnp.where(y_index >= 1, x_index * GY + y_index - 1, -1), jnp.where(y_index < GY - 1, x_index * GY + y_index + 1, -1)]).astype(jnp.int32)
    scores = jax.random.randint(key, (4, GX, GY), 0, 2 ** 20) * 4 + jnp.arange(4, dtype=jnp.int32)[:, None, None]
    ranking = jnp.argsort(scores, axis=0, stable=True)
    return jnp.take_along_axis(neighbour_ids, ranking, axis=0).astype(jnp.int32)


def set_ends(array, rng, smallest, high):
    shape = array.shape
    index_at = [jax.random.randint(jax.random.fold_in(rng, axis), (), 0, shape[axis]) for axis in range(len(shape))]
    array = array.at[tuple(index_at)].set(smallest)
    longest = shape.index(max(shape))
    index_at[longest] = (index_at[longest] + 1) % shape[longest]
    return array.at[tuple(index_at)].set(high)


def shard_levels(own_key, dims, shards, smallest, top_value):
    factor_of = 1.0
    for dim, blocks in shards:
        draws = jax.random.uniform(jax.random.fold_in(jax.random.fold_in(own_key, 6), dim), (blocks,), jnp.float32, smallest / len(shards), top_value / len(shards))
        factor_of = factor_of * jnp.repeat(jnp.exp(draws), dims[dim] // blocks).reshape((-1,) + (1,) * (len(dims) - 1 - dim))
    return factor_of


def deal_out(key, own, number, rows, number_of, top, bound, skew):
    order = jax.random.permutation(key, number_of)
    heavy_load, common = portions_of(number_of, rows * top, bound, skew, True), portions_of(number_of, rows * top, bound, skew, False)
    places = jnp.arange(number_of)

    def named(lengths, rotation):
        used = int((lengths > 0).sum())
        fixed = max(1, used // 4)
        passed = fixed + (places - fixed + rotation * (used - fixed)) % max(1, number_of - fixed)
        return jnp.zeros((number_of,), jnp.int32).at[order[jnp.where(places < fixed, places, passed)]].set(jnp.asarray(lengths, jnp.int32))

    lengths = jnp.where(number % 4 == 0, named(heavy_load, number // 4), named(common, number - number // 4 - 1))
    mixed = jax.random.permutation(jax.random.fold_in(own, 3), number_of)
    source_of, taker = mixed[0:number_of // 2 * 2:2], mixed[1:number_of // 2 * 2:2]
    margin = jnp.minimum(lengths[source_of] - 1, bound - lengths[taker]) // 2
    margin = jnp.where((source_of == order[0]) | (taker == order[0]) | (lengths[taker] == 0), 0, jnp.maximum(margin, 0))
    passed = jax.random.randint(jax.random.fold_in(own, 4), (number_of // 2,), 0, 1 << 20) % (margin + 1)
    lengths = lengths.at[source_of].add(-passed).at[taker].add(passed)
    members = jnp.searchsorted(jnp.cumsum(lengths), jnp.arange(rows * top), side="right").astype(jnp.int32)
    grid = members.reshape(top, rows).T
    grid = grid[jax.random.permutation(jax.random.fold_in(own, 1), rows)]
    rotation = jax.random.randint(jax.random.fold_in(own, 2), (rows, 1), 0, top)
    return jnp.take_along_axis(grid, (jnp.arange(top)[None, :] + rotation) % top, axis=1)


def portions_of(number_of, total, limit, skew, full):
    loads = [(1 << 20) // math.isqrt(rank ** skew) + 1 for rank in range(1, number_of + 1)]
    largest = limit if full else min(limit, max(-(-total // number_of), total * loads[0] // sum(loads)))
    least = 1 if total - largest >= number_of - 1 else 0
    counts, spare = [largest] + [least] * (number_of - 1), total - largest - least * (number_of - 1)
    while spare > 0:
        movable = [i for i in range(1, number_of) if counts[i] < largest] or [i for i in range(1, number_of) if counts[i] < limit]
        mass, budget = sum([loads[i] for i in movable]), spare
        for i in movable:
            addition = min(limit - counts[i], max(1, budget * loads[i] // mass), spare)
            counts[i] = counts[i] + addition
            spare = spare - addition
    return np.array(counts)


def centred(own_key, dims, spread, most, shards=(), kind=jnp.bfloat16):
    array = spread * jax.random.normal(own_key, dims, jnp.float32)
    if shards:
        array = array * shard_levels(own_key, dims, shards, -0.22, 0.18)
    return jnp.clip(array, -most, most).astype(kind)


def setup_inputs(seed: int = 0) -> dict:
    arg_keys = jax.random.split(jax.random.key(seed), 12)
    lam_start = centred(arg_keys[0], (P_SIZE, GX, GY), 1.0, 6.0, ((1, 16), (2, 8)), jnp.float32)
    adj_rhs = centred(arg_keys[1], (P_SIZE, GX, GY), 1.0, 6.0, ((1, 16), (2, 8)), jnp.float32)
    a_diag = draw_a_diag(jax.random.fold_in(arg_keys[11], 71), 0)
    a_off = centred(arg_keys[3], (4, P_SIZE, P_SIZE, GX, GY), 0.02, 0.119628906, ((3, 16), (4, 8)))
    cols = draw_cols(jax.random.fold_in(arg_keys[11], 71), 0)
    smoother = draw_smoother(jax.random.fold_in(arg_keys[11], 71), 0)
    forward_u = centred(arg_keys[6], (P_SIZE, GX, GY), 1.0, 6.0, ((1, 16), (2, 8)), jnp.float32)
    density = jnp.clip(jnp.exp(math.log(1.0) - 1.2039728 * jax.random.uniform(arg_keys[7], (P_SIZE, GX, GY), jnp.float32) ** shard_levels(arg_keys[7], (P_SIZE, GX, GY), ((1, 16), (2, 8)), -0.2, 0.2)), 0.3, 1.0)
    owner_dev_keys = jax.random.split(jax.random.fold_in(arg_keys[8], 1), N_GX * N_GY * NB // NB)
    owner_dev_turns = jax.random.permutation(jax.random.fold_in(arg_keys[8], 3), N_GX * N_GY * NB // NB)
    owner_dev = jax.vmap(lambda own, number: deal_out(jax.random.fold_in(arg_keys[8], 2), own, number, NB, DEVICES, R, CAP, 2))(owner_dev_keys, owner_dev_turns).reshape((N_GX, N_GY, NB, R))
    owner_slot = set_ends(jax.random.randint(arg_keys[9], (N_GX, N_GY, NB, R), 0, NB), jax.random.fold_in(arg_keys[9], 1), 0, NB - 1).astype(jnp.int32)
    filt_weight = jnp.clip(jnp.exp(math.log(1.0) - 1.609438 * jax.random.uniform(arg_keys[10], (N_GX, N_GY, NB, R), jnp.float32) ** shard_levels(arg_keys[10], (N_GX, N_GY, NB, R), ((0, 16), (1, 8)), -0.2, 0.2)), 0.2, 1.0)
    return {"lam_start": lam_start, "adj_rhs": adj_rhs, "a_diag": a_diag, "a_off": a_off, "cols": cols, "smoother": smoother, "forward_u": forward_u, "density": density, "owner_dev": owner_dev, "owner_slot": owner_slot, "filt_weight": filt_weight}


def neighbour_fields(values, cols):
    padded = jnp.pad(values, ((0, 0), (1, 1), (1, 1)))
    shifted = jnp.stack([padded[:, 0:GX, 1:-1], padded[:, 2:, 1:-1], padded[:, 1:-1, 0:GY], padded[:, 1:-1, 2:]])
    x_index = jnp.arange(GX, dtype=jnp.int32)[:, None]
    y_index = jnp.arange(GY, dtype=jnp.int32)[None, :]
    expects = jnp.stack([
        jnp.where(x_index >= 1, (x_index - 1) * GY + y_index, -5),
        jnp.where(x_index < GX - 1, (x_index + 1) * GY + y_index, -5),
        jnp.where(y_index >= 1, x_index * GY + y_index - 1, -5),
        jnp.where(y_index < GY - 1, x_index * GY + y_index + 1, -5)]).astype(jnp.int32)
    matches = (cols[:, None] == expects[None]).astype(jnp.float32)
    return jnp.sum(matches[:, :, None] * shifted[None], axis=1)


def apply_rows(blocks, vectors):
    def one_row(position):
        piece_rows = lax.dynamic_slice_in_dim(blocks, position, 1, 3).astype(jnp.float32)
        vector_rows = lax.dynamic_slice_in_dim(vectors, position, 1, 2)
        return jnp.sum(piece_rows * vector_rows[:, None], axis=(0, 2))[:, 0, :]
    row_results = lax.map(one_row, jnp.arange(blocks.shape[3], dtype=jnp.int32))
    return jnp.transpose(row_results, (1, 0, 2))


def to_rows(values):
    return jnp.transpose(values.reshape(P_SIZE, N_GX, BX, N_GY, BY), (1, 3, 2, 4, 0)).reshape(N_GX * N_GY * NB, P_SIZE)


def from_rows(values):
    shaped = jnp.transpose(values.reshape(N_GX, N_GY, BX, BY, P_SIZE), (4, 0, 2, 1, 3))
    return shaped.reshape(P_SIZE, GX, GY)


def reference(lam_start, adj_rhs, a_diag, a_off, cols, smoother, forward_u, density, owner_dev, owner_slot, filt_weight):
    adjoint = lam_start
    for sweep in range(SWEEPS):
        operator = apply_rows(a_diag[None], adjoint[None]) + apply_rows(a_off, neighbour_fields(adjoint, cols))
        residual = adj_rhs - operator
        adjoint = adjoint + apply_rows(smoother[None], residual[None])
    weighted = (-3.0 * density * density * density) * adjoint * forward_u
    value_rows = to_rows(weighted)
    density_rows = to_rows(density)
    target = (owner_dev * NB + owner_slot).reshape(-1, R)
    weights = filt_weight.reshape(-1, R)
    contrib = (weights[:, :, None] * value_rows[:, None, :]).reshape(-1, P_SIZE)
    numerator = jax.ops.segment_sum(contrib, target.reshape(-1), num_segments=DEVICES * NB)
    weight_total = jax.ops.segment_sum(weights.reshape(-1), target.reshape(-1), num_segments=DEVICES * NB)
    result_rows = (value_rows + numerator) / (density_rows * (1.0 + weight_total[:, None]))
    return adjoint, from_rows(result_rows)
```

```python
import jax
import jax.numpy as jnp
from jax import lax
from jax.experimental import pallas as pl
from jax.experimental.pallas import tpu as pltpu
from jax.sharding import PartitionSpec as P

SWEEPS = 3
F32 = jnp.float32
BF16 = jnp.bfloat16
MESH = pl.DeviceIdType.MESH
NN = (((1,), (0,)), ((), ()))


def merge4(accs, row):
    def step(p, q, mask, shift):
        return jnp.where(mask, p, q) + pltpu.roll(jnp.where(mask, q, p), shift, 0)

    low = (row % 4) < 2
    first = step(accs[0], accs[1], low, 6)
    second = step(accs[2], accs[3], low, 6)
    return step(first, second, row < 4, 4)


def matvec(pairs, write, group, unroll):
    row = lax.broadcasted_iota(jnp.int32, (8, 128), 0)

    def body(g, carry):
        accs = [None] * group
        for blocks, vector in pairs:
            for t in range(8):
                v = vector[16 * t : 16 * t + 16, :]
                for q in range(group):
                    p = blocks[g * group + q, 16 * t : 16 * t + 16, :].astype(F32) * v
                    accs[q] = p[:8] + p[8:] if accs[q] is None else (accs[q] + p[:8]) + p[8:]
        for h in range(group // 4):
            write(g * (group // 4) + h, merge4(accs[4 * h : 4 * h + 4], row))
        return carry

    lax.fori_loop(0, 64 // group, body, 0, unroll=unroll)


def eight(t):
    return pl.ds(pl.multiple_of(t * 8, 8), 8)


def kernel(
    lam_hbm, rhs_hbm, diag_hbm, off_hbm, cols_hbm, smooth_hbm, fu_hbm, dens_hbm, odev_hbm, oslot_hbm, fw_hbm,
    adj_out, filt_out,
    adj, rhs, diag, off, smooth, cols, fu, dens, odev, oslot, fw,
    res, nb, hxs, hxr, hys, hyr, own, route_send, route_near, route_far, far_in, onehot, xg, dens2, ps, pr, filt,
    in_sem, out_sem, hx_send, hx_recv, hy_send, hy_recv, rt_send, rt_recv, fr_sem, xg_send, xg_recv, xf_send, xf_recv,
    rs_send, rs_recv,
):
    ix = lax.axis_index("gx")
    iy = lax.axis_index("gy")
    half = ix // 2
    core = ix % 2
    partner = half * 2 + 1 - core

    def gy_peer(o):
        return (ix, lax.rem(iy + o, 8))

    def gx_peer(o):
        return (lax.rem(half + o, 8) * 2 + core, iy)

    right = lax.rem(ix + 1, 16)
    left = lax.rem(ix + 15, 16)

    sources = [
        (lam_hbm, adj), (odev_hbm, odev), (oslot_hbm, oslot), (fw_hbm, fw), (cols_hbm, cols), (rhs_hbm, rhs),
        (diag_hbm, diag), (off_hbm.at[0], off.at[0]), (off_hbm.at[1], off.at[1]), (off_hbm.at[2], off.at[2]),
        (off_hbm.at[3], off.at[3]), (smooth_hbm, smooth), (fu_hbm, fu), (dens_hbm, dens),
    ]
    loads = [pltpu.make_async_copy(a, b, in_sem.at[n]) for n, (a, b) in enumerate(sources)]
    for load in loads:
        load.start()

    barrier = pltpu.get_barrier_semaphore()
    for o in range(1, 8):
        pl.semaphore_signal(barrier, inc=1, device_id=gy_peer(o), device_id_type=MESH)
        pl.semaphore_signal(barrier, inc=1, device_id=gx_peer(o), device_id_type=MESH)
    for x in (right, left):
        pl.semaphore_signal(barrier, inc=1, device_id=(x, iy), device_id_type=MESH)

    row = lax.broadcasted_iota(jnp.int32, (8, 128), 0)
    lane = lax.broadcasted_iota(jnp.int32, (8, 128), 1)
    odd = (row % 2) == 1
    even = (row % 2) == 0

    def remote(src, dst, send, recv, device):
        return pltpu.make_async_remote_copy(
            src_ref=src, dst_ref=dst, send_sem=send, recv_sem=recv, device_id=device, device_id_type=MESH
        )

    def halo_copies(n):
        return [
            remote(hxs.at[n, 0], hxr.at[n, 0], hx_send.at[n, 0], hx_recv.at[n, 0], (right, iy)),
            remote(hxs.at[n, 1], hxr.at[n, 1], hx_send.at[n, 1], hx_recv.at[n, 1], (left, iy)),
            remote(hys.at[n, 0], hyr.at[n, 0], hy_send.at[n, 0], hy_recv.at[n, 0], gy_peer(1)),
            remote(hys.at[n, 1], hyr.at[n, 1], hy_send.at[n, 1], hy_recv.at[n, 1], gy_peer(7)),
        ]

    def halo_pack(n):
        up = jnp.zeros((8, 128), F32)
        down = jnp.zeros((8, 128), F32)
        for t in range(16):
            v = adj[8 * t : 8 * t + 8, :]
            up = jnp.where(lane == t, pltpu.roll(v, t + 1, 1), up)
            down = jnp.where(lane == t, pltpu.roll(v, t, 1) if t else v, down)
        hys[n, 0] = up
        hys[n, 1] = down
        for t in range(8):
            v, w = adj[8 * t : 8 * t + 8, :], adj[64 + 8 * t : 72 + 8 * t, :]
            hxs[n, 0, 8 * t : 8 * t + 8, :] = jnp.where(odd, v, pltpu.roll(w, 7, 0))
            hxs[n, 1, 8 * t : 8 * t + 8, :] = jnp.where(even, v, pltpu.roll(w, 1, 0))

    def neighbours(n):
        x = ix * 2 + row % 2
        y = iy * 128 + lane
        here = x * 1024 + y
        expects = [
            jnp.where(x >= 1, here - 1024, -5),
            jnp.where(x < 31, here + 1024, -5),
            jnp.where(y >= 1, here - 1, -5),
            jnp.where(y < 1023, here + 1, -5),
        ]
        named = [jnp.concatenate([cols[k]] * 4, axis=0) for k in range(4)]
        match = [[named[k] == e for e in expects] for k in range(4)]
        below, above = hyr[n, 0], hyr[n, 1]
        for t in range(16):
            v = adj[8 * t : 8 * t + 8, :]
            u = t % 8
            lo, hi = hxr[n, 0, 8 * u : 8 * u + 8, :], hxr[n, 1, 8 * u : 8 * u + 8, :]
            if t < 8:
                lo, hi = pltpu.roll(lo, 7, 0), pltpu.roll(hi, 1, 0)
            shifted = [
                jnp.where(even, lo, pltpu.roll(v, 1, 0)),
                jnp.where(odd, hi, pltpu.roll(v, 7, 0)),
                jnp.where(lane == 0, pltpu.roll(below, (128 - t) % 128, 1) if t else below, pltpu.roll(v, 1, 1)),
                jnp.where(lane == 127, pltpu.roll(above, 127 - t, 1), pltpu.roll(v, 127, 1)),
            ]
            for k in range(4):
                value = jnp.zeros((8, 128), F32)
                for m in range(4):
                    value = jnp.where(match[k][m], shifted[m], value)
                nb[k, 8 * t : 8 * t + 8, :] = value

    def routes(block, carry):
        far, oy = block // 8, block % 8
        to_core = core + far - 2 * core * far
        to_half = (half + lax.broadcasted_iota(jnp.int32, (8, 256), 0)) % 8
        rank = to_half * 16 + to_core * 8 + (iy + oy) % 8
        slot = jnp.full((8, 256), -1, jnp.int32)
        weight = jnp.zeros((8, 256), F32)
        for r in range(16):
            hit = odev[r : r + 1, :] == rank
            slot = jnp.where(hit, oslot[r : r + 1, :], slot)
            weight = jnp.where(hit, fw[r : r + 1, :], weight)
        route_send[far, oy, :8, :] = slot.astype(F32)
        route_send[far, oy, 8:, :] = weight
        return carry

    loads[0].wait()
    for n in (1, 2, 3):
        loads[n].wait()
    halo_pack(0)
    pl.semaphore_wait(barrier, 16)
    for copy in halo_copies(0):
        copy.start()
    lax.fori_loop(0, 16, routes, 0)
    route_near[0] = route_send[0, 0]
    route_far[0] = route_send[1, 0]

    def route_copies(o):
        return [
            remote(route_send.at[0, o], route_near.at[o], rt_send.at[0, o], rt_recv.at[0, o], gy_peer(o)),
            remote(route_send.at[1, o], route_far.at[o], rt_send.at[1, o], rt_recv.at[1, o], gy_peer(o)),
        ]

    for o in range(1, 8):
        for copy in route_copies(o):
            copy.start()
    route_forward = remote(route_far, far_in, fr_sem.at[0], fr_sem.at[1], (partner, iy))

    def start_residual(t, x):
        res[eight(t), :] = rhs[eight(t), :] - x

    def lower_residual(t, x):
        res[eight(t), :] = res[eight(t), :] - x

    def raise_adjoint(t, x):
        adj[eight(t), :] = adj[eight(t), :] + x

    column = lax.broadcasted_iota(jnp.int32, (256, 256), 1).astype(F32).astype(BF16)

    def build(table, base):
        def body(s, carry):
            slots = jnp.transpose(table[s, :8, :]).astype(BF16)
            for d in range(8):
                hit = jnp.broadcast_to(slots[:, d : d + 1], (256, 256)) == column
                onehot[base + s, d] = jnp.where(hit, BF16(1), BF16(0))
            return carry

        lax.fori_loop(0, 8, body, 0)

    for n in range(SWEEPS):
        if n:
            halo_pack(n)
            for copy in halo_copies(n):
                copy.start()
        else:
            loads[4].wait()
            loads[5].wait()
            loads[6].wait()
        matvec([(diag, adj)], start_residual, 8, 1)
        if n == 1:
            build(route_near, 0)
        if n == 2:
            build(far_in, 8)
        for copy in halo_copies(n):
            copy.wait_recv()
        neighbours(n)
        if n == 0:
            for k in range(4):
                loads[7 + k].wait()
                matvec([(off.at[k], nb.at[k])], lower_residual, 8, 1)
            loads[11].wait()
            for o in range(1, 8):
                for copy in route_copies(o):
                    copy.wait_recv()
            route_forward.start()
        else:
            matvec([(off.at[k], nb.at[k]) for k in range(4)], lower_residual, 4, 2)
        if n == 1:
            route_forward.wait_recv()
        matvec([(smooth, res)], raise_adjoint, 8, 1)

    loads[12].wait()
    loads[13].wait()
    adj_copy = pltpu.make_async_copy(adj, adj_out, out_sem.at[0])
    adj_copy.start()
    d = dens[...]
    own[...] = -3.0 * d * d * d * adj[...] * fu[...]
    for b in range(2):
        xg[0, :, 128 * b : 128 * b + 128] = own[pl.ds(b, 64, 2), :]
        dens2[:, 128 * b : 128 * b + 128] = dens[pl.ds(b, 64, 2), :]

    spread = {
        o: remote(xg.at[0], xg.at[o], xg_send.at[o], xg_recv.at[o], gy_peer(o)) for o in range(1, 8)
    }
    passed = [remote(xg.at[o], xg.at[8 + o], xf_send.at[o], xf_recv.at[o], (partner, iy)) for o in range(8)]
    for o in (4, 3, 5, 2, 6, 1, 7):
        spread[o].start()
    passed[0].start()
    for o in (1, 7, 2, 6, 3, 5, 4):
        spread[o].wait_recv()
        passed[o].start()
    for o in range(8):
        passed[o].wait_recv()

    def partial(d):
        acc = jnp.zeros((144, 256), F32)
        for s in range(16):
            table = route_near if s < 8 else far_in
            w = table[s % 8, pl.ds(8 + d, 1), :]
            p = xg[s] * w
            top = p.astype(BF16)
            rest = (p - top.astype(F32)).astype(BF16)
            w16 = jnp.broadcast_to(w, (16, 256))
            wtop = w16.astype(BF16).astype(F32)
            r16 = lax.broadcasted_iota(jnp.int32, (16, 256), 0)
            tail = jnp.where(r16 == 0, wtop, jnp.where(r16 == 1, w16 - wtop, 0.0)).astype(BF16)
            lhs = jnp.concatenate([top, rest, tail], axis=0)
            acc += lax.dot_general(lhs, onehot[s, d], NN, preferred_element_type=F32)
        weights = acc[128:136] + pltpu.roll(acc[128:136], 7, 0)
        return acc[:64] + acc[64:128], weights

    def reduce_copy(d):
        return remote(ps.at[d], pr.at[d], rs_send.at[d], rs_recv.at[d], gx_peer(d))

    def send_partial(d, carry):
        values, weights = partial(d)
        ps[d, :64] = values
        ps[d, 64:] = weights
        reduce_copy(d).start()
        return carry

    lax.fori_loop(1, 8, send_partial, 0)
    values, weights = partial(0)
    for d in range(1, 8):
        reduce_copy(d).wait_recv()
    for d in range(1, 8):
        values += pr[d, :64]
        weights += pr[d, 64:]
    total = weights[0:1]
    result = (xg[0] + values) / (dens2[...] * (1.0 + total))
    for b in range(2):
        filt[pl.ds(b, 64, 2), :] = result[:, 128 * b : 128 * b + 128]
    filt_copy = pltpu.make_async_copy(filt, filt_out, out_sem.at[1])
    filt_copy.start()

    for n in range(SWEEPS):
        for copy in halo_copies(n):
            copy.wait_send()
    for o in range(1, 8):
        for copy in route_copies(o):
            copy.wait_send()
        spread[o].wait_send()
        reduce_copy(o).wait_send()
    for copy in passed:
        copy.wait_send()
    route_forward.wait_send()
    adj_copy.wait()
    filt_copy.wait()


def local(lam_start, adj_rhs, a_diag, a_off, cols, smoother, forward_u, density, owner_dev, owner_slot, filt_weight):
    width, rows_x, rows_y = lam_start.shape
    rows = width * rows_x

    def by_row(x):
        return x.reshape(x.shape[:-3] + (rows, rows_y))

    def by_owner(x):
        return jnp.transpose(x, (0, 1, 3, 2)).reshape(x.shape[3], x.shape[2])

    any_spec = pl.BlockSpec(memory_space=pl.ANY)
    dma = pltpu.SemaphoreType.DMA
    vm = pltpu.VMEM
    adjoint, filtered = pl.pallas_call(
        kernel,
        out_shape=[jax.ShapeDtypeStruct((rows, rows_y), F32)] * 2,
        in_specs=[any_spec] * 11,
        out_specs=[any_spec] * 2,
        scratch_shapes=[
            vm((128, 128), F32), vm((128, 128), F32), vm((64, 128, 128), BF16), vm((4, 64, 128, 128), BF16),
            vm((64, 128, 128), BF16), vm((4, 2, 128), jnp.int32), vm((128, 128), F32), vm((128, 128), F32),
            vm((16, 256), jnp.int32), vm((16, 256), jnp.int32), vm((16, 256), F32),
            vm((128, 128), F32), vm((4, 128, 128), F32), vm((3, 2, 64, 128), F32), vm((3, 2, 64, 128), F32),
            vm((3, 2, 8, 128), F32), vm((3, 2, 8, 128), F32), vm((128, 128), F32),
            vm((2, 8, 16, 256), F32), vm((8, 16, 256), F32), vm((8, 16, 256), F32), vm((8, 16, 256), F32),
            vm((16, 8, 256, 256), BF16), vm((16, 64, 256), F32), vm((64, 256), F32),
            vm((8, 72, 256), F32), vm((8, 72, 256), F32), vm((128, 128), F32),
            dma((14,)), dma((2,)), dma((3, 2)), dma((3, 2)), dma((3, 2)), dma((3, 2)), dma((2, 8)), dma((2, 8)),
            dma((2,)), dma((8,)), dma((8,)), dma((8,)), dma((8,)), dma((8,)), dma((8,)),
        ],
        compiler_params=pltpu.CompilerParams(
            collective_id=0, has_side_effects=True, vmem_limit_bytes=56 * 2**20
        ),
        name="sweeps_and_filter",
    )(
        by_row(lam_start), by_row(adj_rhs), by_row(a_diag), by_row(a_off), cols, by_row(smoother),
        by_row(forward_u), by_row(density), by_owner(owner_dev), by_owner(owner_slot), by_owner(filt_weight),
    )
    shape = (width, rows_x, rows_y)
    return adjoint.reshape(shape), filtered.reshape(shape)


def solution(mesh):
    in_specs = (
        P(None, "gx", "gy"),
        P(None, "gx", "gy"),
        P(None, None, "gx", "gy"),
        P(None, None, None, "gx", "gy"),
        P(None, "gx", "gy"),
        P(None, None, "gx", "gy"),
        P(None, "gx", "gy"),
        P(None, "gx", "gy"),
        P("gx", "gy", None, None),
        P("gx", "gy", None, None),
        P("gx", "gy", None, None),
    )
    out_specs = (P(None, "gx", "gy"), P(None, "gx", "gy"))
    return jax.shard_map(local, mesh=mesh, in_specs=in_specs, out_specs=out_specs, check_vma=False)
```

```python
import jax
import jax.numpy as jnp
from jax import lax
from jax.experimental import pallas as pl
from jax.experimental.pallas import tpu as pltpu
from jax.sharding import PartitionSpec as P

SWEEPS = 3
F32 = jnp.float32
BF16 = jnp.bfloat16
MESH = pl.DeviceIdType.MESH
NN = (((1,), (0,)), ((), ()))
AHEAD = 2


def merge4(accs, row):
    def step(p, q, mask, shift):
        return jnp.where(mask, p, q) + pltpu.roll(jnp.where(mask, q, p), shift, 0)

    low = (row % 4) < 2
    first = step(accs[0], accs[1], low, 6)
    second = step(accs[2], accs[3], low, 6)
    return step(first, second, row < 4, 4)


def matvec(pairs, write, group, unroll):
    row = lax.broadcasted_iota(jnp.int32, (8, 128), 0)

    def body(g, carry):
        accs = [None] * group
        for blocks, vector in pairs:
            for t in range(8):
                v = vector[16 * t : 16 * t + 16, :]
                for q in range(group):
                    p = blocks[g * group + q, 16 * t : 16 * t + 16, :].astype(F32) * v
                    accs[q] = p[:8] + p[8:] if accs[q] is None else (accs[q] + p[:8]) + p[8:]
        for h in range(group // 4):
            write(g * (group // 4) + h, merge4(accs[4 * h : 4 * h + 4], row))
        return carry

    lax.fori_loop(0, 64 // group, body, 0, unroll=unroll)


def eight(t):
    return pl.ds(pl.multiple_of(t * 8, 8), 8)


def kernel(
    lam_hbm, rhs_hbm, diag_hbm, off_hbm, cols_hbm, smooth_hbm, fu_hbm, dens_hbm, odev_hbm, oslot_hbm, fw_hbm,
    adj_out, filt_out,
    adj, rhs, diag, off, smooth, cols, fu, dens, odev, oslot, fw,
    res, nb, off_x, off_y, halo, hxs, hxr, hys, hyr, own, route_send, route_near, route_far, onehot, xg, dens2, factor, cs, cr, ps, pr, filt,
    in_sem, out_sem, hx_send, hx_recv, hy_send, hy_recv, rt_send, rt_recv, xg_send, xg_recv, xc_send, xc_recv,
    rs_send, rs_recv,
):
    ix = lax.axis_index("gx")
    iy = lax.axis_index("gy")
    half = ix // 2
    core = ix % 2
    partner = half * 2 + 1 - core

    def gy_peer(o):
        return (ix, lax.rem(iy + o, 8))

    def gx_peer(o):
        return (lax.rem(half + o, 8) * 2 + core, iy)

    right = lax.rem(ix + 1, 16)
    left = lax.rem(ix + 15, 16)

    sources = [
        (lam_hbm, adj), (odev_hbm, odev), (oslot_hbm, oslot), (fw_hbm, fw), (cols_hbm, cols), (rhs_hbm, rhs),
        (diag_hbm, diag), (off_hbm.at[0], off.at[0]), (off_hbm.at[1], off.at[1]), (off_hbm.at[2], off.at[2]),
        (off_hbm.at[3], off.at[3]), (smooth_hbm, smooth), (fu_hbm, fu), (dens_hbm, dens),
    ]
    loads = [pltpu.make_async_copy(a, b, in_sem.at[n]) for n, (a, b) in enumerate(sources)]
    for load in loads:
        load.start()

    barrier = pltpu.get_barrier_semaphore()
    for o in range(1, 8):
        pl.semaphore_signal(barrier, inc=1, device_id=gy_peer(o), device_id_type=MESH)
        pl.semaphore_signal(barrier, inc=1, device_id=gx_peer(o), device_id_type=MESH)
    for x in (right, left):
        pl.semaphore_signal(barrier, inc=1, device_id=(x, iy), device_id_type=MESH)

    row = lax.broadcasted_iota(jnp.int32, (8, 128), 0)
    lane = lax.broadcasted_iota(jnp.int32, (8, 128), 1)
    odd = (row % 2) == 1
    even = (row % 2) == 0

    def remote(src, dst, send, recv, device):
        return pltpu.make_async_remote_copy(
            src_ref=src, dst_ref=dst, send_sem=send, recv_sem=recv, device_id=device, device_id_type=MESH
        )

    def halo_copies(n):
        return [
            remote(hxs.at[n, 0], hxr.at[n, 0], hx_send.at[n, 0], hx_recv.at[n, 0], (right, iy)),
            remote(hxs.at[n, 1], hxr.at[n, 1], hx_send.at[n, 1], hx_recv.at[n, 1], (left, iy)),
            remote(hys.at[n, 0], hyr.at[n, 0], hy_send.at[n, 0], hy_recv.at[n, 0], gy_peer(1)),
            remote(hys.at[n, 1], hyr.at[n, 1], hy_send.at[n, 1], hy_recv.at[n, 1], gy_peer(7)),
        ]

    def pack_x(n):
        for t in range(8):
            v, w = adj[8 * t : 8 * t + 8, :], adj[64 + 8 * t : 72 + 8 * t, :]
            hxs[n, 0, 8 * t : 8 * t + 8, :] = jnp.where(odd, v, pltpu.roll(w, 7, 0))
            hxs[n, 1, 8 * t : 8 * t + 8, :] = jnp.where(even, v, pltpu.roll(w, 1, 0))

    def pack_y(n):
        up = jnp.zeros((8, 128), F32)
        down = jnp.zeros((8, 128), F32)
        for t in range(16):
            v = adj[8 * t : 8 * t + 8, :]
            up = jnp.where(lane == t, pltpu.roll(v, t + 1, 1), up)
            down = jnp.where(lane == t, pltpu.roll(v, t, 1) if t else v, down)
        hys[n, 0] = up
        hys[n, 1] = down

    def matches():
        x = ix * 2 + row % 2
        y = iy * 128 + lane
        here = x * 1024 + y
        expects = [
            jnp.where(x >= 1, here - 1024, -5),
            jnp.where(x < 31, here + 1024, -5),
            jnp.where(y >= 1, here - 1, -5),
            jnp.where(y < 1023, here + 1, -5),
        ]
        named = [jnp.concatenate([cols[k]] * 4, axis=0) for k in range(4)]
        return [[named[k] == e for e in expects] for k in range(4)]

    def inner_neighbours():
        match = matches()
        zero = jnp.zeros((8, 128), F32)
        keep = [odd, even, lane > 0, lane < 127]
        masks = [[match[k][m] & keep[m] for m in range(4)] for k in range(4)]
        for t in range(16):
            v = adj[8 * t : 8 * t + 8, :]
            shifted = [pltpu.roll(v, 1, 0), pltpu.roll(v, 7, 0), pltpu.roll(v, 1, 1), pltpu.roll(v, 127, 1)]
            for k in range(4):
                value = zero
                for m in range(4):
                    value = jnp.where(masks[k][m], shifted[m], value)
                nb[k, 8 * t : 8 * t + 8, :] = value

    def gather_outer():
        match = matches()
        none = jnp.full((8, 128), 9.0, F32)
        along_x, along_y = none, none
        for k in range(4):
            along_x = jnp.where((even & match[k][0]) | (odd & match[k][1]), float(k), along_x)
            first, last = match[k][2] & (lane == 0), match[k][3] & (lane == 127)
            along_y = jnp.where(first | last, float(k), along_y)
        pick_x = jnp.concatenate([along_x] * 2, axis=0).astype(BF16)
        pick_y = jnp.concatenate([along_y] * 2, axis=0).astype(BF16)

        def body(i, carry):
            for t in range(8):
                rows = slice(16 * t, 16 * t + 16)
                a = [off[k, i, rows, :] for k in range(4)]
                for pick, out in ((pick_x, off_x), (pick_y, off_y)):
                    value = jnp.zeros((16, 128), BF16)
                    for k in range(4):
                        value = jnp.where(pick == BF16(k), a[k], value)
                    out[i, rows, :] = value
            return carry

        lax.fori_loop(0, 64, body, 0)

    def outer_x(n):
        for t in range(8):
            lo, hi = hxr[n, 0, 8 * t : 8 * t + 8, :], hxr[n, 1, 8 * t : 8 * t + 8, :]
            halo[8 * t : 8 * t + 8, :] = jnp.where(even, pltpu.roll(lo, 7, 0), pltpu.roll(hi, 1, 0))
            halo[64 + 8 * t : 72 + 8 * t, :] = jnp.where(even, lo, hi)

    def outer_y(n):
        below, above = hyr[n, 0], hyr[n, 1]
        for t in range(16):
            lo = pltpu.roll(below, 128 - t, 1) if t else below
            halo[8 * t : 8 * t + 8, :] = jnp.where(lane == 0, lo, pltpu.roll(above, 127 - t, 1))

    def routes(block, carry):
        far, oy = block // 8, block % 8
        to_core = core + far - 2 * core * far
        to_half = (half + lax.broadcasted_iota(jnp.int32, (8, 256), 0)) % 8
        rank = to_half * 16 + to_core * 8 + (iy + oy) % 8
        slot = jnp.full((8, 256), -1, jnp.int32)
        weight = jnp.zeros((8, 256), F32)
        for r in range(16):
            hit = odev[r : r + 1, :] == rank
            slot = jnp.where(hit, oslot[r : r + 1, :], slot)
            weight = jnp.where(hit, fw[r : r + 1, :], weight)
        route_send[far, oy, :8, :] = slot.astype(F32)
        route_send[far, oy, 8:, :] = weight
        return carry


    def route_copies(o):
        return [
            remote(route_send.at[0, o], route_near.at[o], rt_send.at[0, o], rt_recv.at[0, o], gy_peer(o)),
            remote(route_send.at[1, o], route_far.at[o], rt_send.at[1, o], rt_recv.at[1, o], gy_peer(o)),
        ]

    def start_residual(t, x):
        res[eight(t), :] = rhs[eight(t), :] - x

    def lower_residual(t, x):
        res[eight(t), :] = res[eight(t), :] - x

    def raise_adjoint(t, x):
        adj[eight(t), :] = adj[eight(t), :] + x

    def inner_off():
        matvec([(off.at[k], nb.at[k]) for k in range(4)], lower_residual, 4, 2)

    column = lax.broadcasted_iota(jnp.int32, (256, 256), 1).astype(F32).astype(BF16)

    def build(table, base):
        def body(s, carry):
            slots = jnp.transpose(table[s, :8, :]).astype(BF16)
            for d in range(8):
                hit = jnp.broadcast_to(slots[:, d : d + 1], (256, 256)) == column
                onehot[base + s, d] = jnp.where(hit, BF16(1), BF16(0))
            return carry

        lax.fori_loop(0, 8, body, 0)

    loads[0].wait()
    pack_x(0)
    pack_y(0)
    for n in (1, 2, 3):
        loads[n].wait()
    lax.fori_loop(0, 16, routes, 0)
    route_near[0] = route_send[0, 0]
    route_far[0] = route_send[1, 0]
    pl.semaphore_wait(barrier, 16)
    for copy in halo_copies(0):
        copy.start()
    for n in (4, 5, 6):
        loads[n].wait()
    matvec([(diag, adj)], start_residual, 8, 1)
    inner_neighbours()
    for k in range(4):
        loads[7 + k].wait()
    gather_outer()
    inner_off()
    loads[11].wait()
    loads[12].wait()
    loads[13].wait()
    d = dens[...]
    factor[...] = -3.0 * d * d * d * fu[...]
    for b in range(2):
        dens2[:, 128 * b : 128 * b + 128] = dens[pl.ds(b, 64, 2), :]

    for n in range(SWEEPS):
        copies = halo_copies(n)
        if n:
            pack_x(n)
            copies[0].start()
            copies[1].start()
            pack_y(n)
            copies[2].start()
            copies[3].start()
            matvec([(diag, adj)], start_residual, 8, 1)
            inner_neighbours()
            inner_off()
        copies[2].wait_recv()
        copies[3].wait_recv()
        outer_y(n)
        matvec([(off_y, halo)], lower_residual, 8, 1)
        copies[0].wait_recv()
        copies[1].wait_recv()
        if n == 0:
            for o in range(1, 8):
                for copy in route_copies(o):
                    copy.start()
        outer_x(n)
        matvec([(off_x, halo)], lower_residual, 8, 1)
        matvec([(smooth, res)], raise_adjoint, 8, 1)

    adj_copy = pltpu.make_async_copy(adj, adj_out, out_sem.at[0])
    adj_copy.start()
    own[...] = factor[...] * adj[...]
    for b in range(2):
        xg[0, :, 128 * b : 128 * b + 128] = own[pl.ds(b, 64, 2), :]

    spread = {
        o: remote(xg.at[0], xg.at[o], xg_send.at[o], xg_recv.at[o], gy_peer(o)) for o in range(1, 8)
    }
    for o in (4, 3, 5, 1, 7, 2, 6):
        spread[o].start()
    for o in range(1, 8):
        for copy in route_copies(o):
            copy.wait_recv()
    build(route_far, 8)
    build(route_near, 0)

    def partial(far, d):
        table = route_far if far else route_near
        out = jnp.zeros((144, 256), F32)
        for o in range(8):
            w = table[o, pl.ds(8 + d, 1), :]
            p = xg[o] * w
            top = p.astype(BF16)
            rest = (p - top.astype(F32)).astype(BF16)
            w16 = jnp.broadcast_to(w, (16, 256))
            wtop = w16.astype(BF16).astype(F32)
            r16 = lax.broadcasted_iota(jnp.int32, (16, 256), 0)
            tail = jnp.where(r16 == 0, wtop, jnp.where(r16 == 1, w16 - wtop, 0.0)).astype(BF16)
            lhs = jnp.concatenate([top, rest, tail], axis=0)
            out += lax.dot_general(lhs, onehot[8 * far + o, d], NN, preferred_element_type=F32)
        return out[:64] + out[64:128], out[128:136] + pltpu.roll(out[128:136], 7, 0)

    def cross_copy(d):
        return remote(cs.at[d], cr.at[d], xc_send.at[d], xc_recv.at[d], (partner, iy))

    def reduce_copy(d):
        return remote(ps.at[d], pr.at[d], rs_send.at[d], rs_recv.at[d], gx_peer(d))

    def turn(k):
        return (3 * k + 3) % 8

    def send_cross(d):
        values, weights = partial(1, d)
        cs[d, :64] = values
        cs[d, 64:] = weights
        cross_copy(d).start()

    def send_partial(k, carry):
        d = turn(k)

        @pl.when(k < 8 - AHEAD)
        def _():
            send_cross(turn(k + AHEAD))

        values, weights = partial(0, d)
        cross_copy(d).wait_recv()
        ps[d, :64] = values + cr[d, :64]
        ps[d, 64:] = weights + cr[d, 64:]
        reduce_copy(d).start()
        return carry

    for o in (2, 6, 1, 7, 4, 3, 5):
        spread[o].wait_recv()
    for k in range(AHEAD):
        send_cross(turn(k))
    lax.fori_loop(0, 7, send_partial, 0)
    values, weights = partial(0, 0)
    cross_copy(0).wait_recv()
    values += cr[0, :64]
    weights += cr[0, 64:]
    for d in (2, 6, 4, 1, 7, 3, 5):
        reduce_copy(d).wait_recv()
        values += pr[d, :64]
        weights += pr[d, 64:]
    total = weights[0:1]
    result = (xg[0] + values) / (dens2[...] * (1.0 + total))
    for b in range(2):
        filt[pl.ds(b, 64, 2), :] = result[:, 128 * b : 128 * b + 128]
    filt_copy = pltpu.make_async_copy(filt, filt_out, out_sem.at[1])
    filt_copy.start()

    for n in range(SWEEPS):
        for copy in halo_copies(n):
            copy.wait_send()
    for o in range(1, 8):
        for copy in route_copies(o):
            copy.wait_send()
        spread[o].wait_send()
        reduce_copy(o).wait_send()
    for d in range(8):
        cross_copy(d).wait_send()
    adj_copy.wait()
    filt_copy.wait()


def hand_over(a, b, a_out, b_out):
    a_out[...] = a[...]
    b_out[...] = b[...]


def local(lam_start, adj_rhs, a_diag, a_off, cols, smoother, forward_u, density, owner_dev, owner_slot, filt_weight):
    width, rows_x, rows_y = lam_start.shape
    rows = width * rows_x

    def by_row(x):
        return x.reshape(x.shape[:-3] + (rows, rows_y))

    def by_owner(x):
        return jnp.transpose(x, (0, 1, 3, 2)).reshape(x.shape[3], x.shape[2])

    any_spec = pl.BlockSpec(memory_space=pl.ANY)
    dma = pltpu.SemaphoreType.DMA
    vm = pltpu.VMEM
    adjoint, filtered = pl.pallas_call(
        kernel,
        out_shape=[jax.ShapeDtypeStruct((rows, rows_y), F32)] * 2,
        in_specs=[any_spec] * 11,
        out_specs=[any_spec] * 2,
        scratch_shapes=[
            vm((128, 128), F32), vm((128, 128), F32), vm((64, 128, 128), BF16), vm((4, 64, 128, 128), BF16),
            vm((64, 128, 128), BF16), vm((4, 2, 128), jnp.int32), vm((128, 128), F32), vm((128, 128), F32),
            vm((16, 256), jnp.int32), vm((16, 256), jnp.int32), vm((16, 256), F32),
            vm((128, 128), F32), vm((4, 128, 128), F32), vm((64, 128, 128), BF16), vm((64, 128, 128), BF16),
            vm((128, 128), F32), vm((3, 2, 64, 128), F32), vm((3, 2, 64, 128), F32),
            vm((3, 2, 8, 128), F32), vm((3, 2, 8, 128), F32), vm((128, 128), F32),
            vm((2, 8, 16, 256), F32), vm((8, 16, 256), F32), vm((8, 16, 256), F32),
            vm((16, 8, 256, 256), BF16), vm((8, 64, 256), F32), vm((64, 256), F32), vm((128, 128), F32),
            vm((8, 72, 256), F32), vm((8, 72, 256), F32),
            vm((8, 72, 256), F32), vm((8, 72, 256), F32), vm((128, 128), F32),
            dma((14,)), dma((2,)), dma((3, 2)), dma((3, 2)), dma((3, 2)), dma((3, 2)), dma((2, 8)), dma((2, 8)),
            dma((8,)), dma((8,)), dma((8,)), dma((8,)), dma((8,)), dma((8,)),
        ],
        compiler_params=pltpu.CompilerParams(
            collective_id=0, has_side_effects=True, vmem_limit_bytes=56 * 2**20
        ),
        name="sweeps_and_filter",
    )(
        by_row(lam_start), by_row(adj_rhs), by_row(a_diag), by_row(a_off), cols, by_row(smoother),
        by_row(forward_u), by_row(density), by_owner(owner_dev), by_owner(owner_slot), by_owner(filt_weight),
    )
    adjoint, filtered = pl.pallas_call(
        hand_over,
        out_shape=[jax.ShapeDtypeStruct((rows, rows_y), F32)] * 2,
        in_specs=[pl.BlockSpec(memory_space=vm)] * 2,
        out_specs=[pl.BlockSpec(memory_space=vm)] * 2,
        name="hand_over",
    )(adjoint, filtered)
    shape = (width, rows_x, rows_y)
    return adjoint.reshape(shape), filtered.reshape(shape)


def solution(mesh):
    in_specs = (
        P(None, "gx", "gy"),
        P(None, "gx", "gy"),
        P(None, None, "gx", "gy"),
        P(None, None, None, "gx", "gy"),
        P(None, "gx", "gy"),
        P(None, None, "gx", "gy"),
        P(None, "gx", "gy"),
        P(None, "gx", "gy"),
        P("gx", "gy", None, None),
        P("gx", "gy", None, None),
        P("gx", "gy", None, None),
    )
    out_specs = (P(None, "gx", "gy"), P(None, "gx", "gy"))
    return jax.shard_map(local, mesh=mesh, in_specs=in_specs, out_specs=out_specs, check_vma=False)
```

```python
import functools

import jax
import jax.numpy as jnp
from jax import lax
from jax.experimental import pallas as pl
from jax.experimental.pallas import tpu as pltpu
from jax.sharding import PartitionSpec as P

SWEEPS = 3
F32 = jnp.float32
BF16 = jnp.bfloat16
MESH = pl.DeviceIdType.MESH
NN = (((1,), (0,)), ((), ()))
AHEAD = 2


def merge4(accs, row):
    def step(p, q, mask, shift):
        return jnp.where(mask, p, q) + pltpu.roll(jnp.where(mask, q, p), shift, 0)

    low = (row % 4) < 2
    first = step(accs[0], accs[1], low, 6)
    second = step(accs[2], accs[3], low, 6)
    return step(first, second, row < 4, 4)


def matvec(pairs, write, group, unroll):
    row = lax.broadcasted_iota(jnp.int32, (8, 128), 0)

    def body(g, carry):
        accs = [None] * group
        for blocks, vector in pairs:
            for t in range(8):
                v = vector[16 * t : 16 * t + 16, :]
                for q in range(group):
                    p = blocks[g * group + q, 16 * t : 16 * t + 16, :].astype(F32) * v
                    accs[q] = p[:8] + p[8:] if accs[q] is None else (accs[q] + p[:8]) + p[8:]
        for h in range(group // 4):
            write(g * (group // 4) + h, merge4(accs[4 * h : 4 * h + 4], row))
        return carry

    lax.fori_loop(0, 64 // group, body, 0, unroll=unroll)


def eight(t):
    return pl.ds(pl.multiple_of(t * 8, 8), 8)


def kernel(
    lam_hbm, rhs_hbm, diag_hbm, off_hbm, cols_hbm, smooth_hbm, fu_hbm, dens_hbm, odev_hbm, oslot_hbm, fw_hbm,
    adj_out, filt_out,
    adj, rhs, diag, off, smooth, cols, fu, dens, odev, oslot, fw,
    res, nb, off_x, off_y, halo, hxs, hxr, hys, hyr, own, route_send, route_near, route_far, onehot, xg, dens2, factor, cs, cr, ps, pr, filt,
    in_sem, out_sem, hx_send, hx_recv, hy_send, hy_recv, rt_send, rt_recv, xg_send, xg_recv, xc_send, xc_recv,
    rs_send, rs_recv,
):
    ix = lax.axis_index("gx")
    iy = lax.axis_index("gy")
    half = ix // 2
    core = ix % 2
    partner = half * 2 + 1 - core

    def gy_peer(o):
        return (ix, lax.rem(iy + o, 8))

    def gx_peer(o):
        return (lax.rem(half + o, 8) * 2 + core, iy)

    right = lax.rem(ix + 1, 16)
    left = lax.rem(ix + 15, 16)

    sources = [
        (lam_hbm, adj), (odev_hbm, odev), (oslot_hbm, oslot), (fw_hbm, fw), (cols_hbm, cols), (rhs_hbm, rhs),
        (diag_hbm, diag), (off_hbm.at[0], off.at[0]), (off_hbm.at[1], off.at[1]), (off_hbm.at[2], off.at[2]),
        (off_hbm.at[3], off.at[3]), (smooth_hbm, smooth), (fu_hbm, fu), (dens_hbm, dens),
    ]
    loads = [pltpu.make_async_copy(a, b, in_sem.at[n]) for n, (a, b) in enumerate(sources)]
    for load in loads:
        load.start()

    barrier = pltpu.get_barrier_semaphore()
    for o in range(1, 8):
        pl.semaphore_signal(barrier, inc=1, device_id=gy_peer(o), device_id_type=MESH)
        pl.semaphore_signal(barrier, inc=1, device_id=gx_peer(o), device_id_type=MESH)
    for x in (right, left):
        pl.semaphore_signal(barrier, inc=1, device_id=(x, iy), device_id_type=MESH)

    row = lax.broadcasted_iota(jnp.int32, (8, 128), 0)
    lane = lax.broadcasted_iota(jnp.int32, (8, 128), 1)
    odd = (row % 2) == 1
    even = (row % 2) == 0

    def remote(src, dst, send, recv, device):
        return pltpu.make_async_remote_copy(
            src_ref=src, dst_ref=dst, send_sem=send, recv_sem=recv, device_id=device, device_id_type=MESH
        )

    def halo_copies(n):
        return [
            remote(hxs.at[n, 0], hxr.at[n, 0], hx_send.at[n, 0], hx_recv.at[n, 0], (right, iy)),
            remote(hxs.at[n, 1], hxr.at[n, 1], hx_send.at[n, 1], hx_recv.at[n, 1], (left, iy)),
            remote(hys.at[n, 0], hyr.at[n, 0], hy_send.at[n, 0], hy_recv.at[n, 0], gy_peer(1)),
            remote(hys.at[n, 1], hyr.at[n, 1], hy_send.at[n, 1], hy_recv.at[n, 1], gy_peer(7)),
        ]

    def pack_x(n):
        for t in range(8):
            v, w = adj[8 * t : 8 * t + 8, :], adj[64 + 8 * t : 72 + 8 * t, :]
            hxs[n, 0, 8 * t : 8 * t + 8, :] = jnp.where(odd, v, pltpu.roll(w, 7, 0))
            hxs[n, 1, 8 * t : 8 * t + 8, :] = jnp.where(even, v, pltpu.roll(w, 1, 0))

    def pack_y(n):
        up = jnp.zeros((8, 128), F32)
        down = jnp.zeros((8, 128), F32)
        for t in range(16):
            v = adj[8 * t : 8 * t + 8, :]
            up = jnp.where(lane == t, pltpu.roll(v, t + 1, 1), up)
            down = jnp.where(lane == t, pltpu.roll(v, t, 1) if t else v, down)
        hys[n, 0] = up
        hys[n, 1] = down

    def matches():
        x = ix * 2 + row % 2
        y = iy * 128 + lane
        here = x * 1024 + y
        expects = [
            jnp.where(x >= 1, here - 1024, -5),
            jnp.where(x < 31, here + 1024, -5),
            jnp.where(y >= 1, here - 1, -5),
            jnp.where(y < 1023, here + 1, -5),
        ]
        named = [jnp.concatenate([cols[k]] * 4, axis=0) for k in range(4)]
        return [[named[k] == e for e in expects] for k in range(4)]

    def inner_neighbours():
        match = matches()
        zero = jnp.zeros((8, 128), F32)
        keep = [odd, even, lane > 0, lane < 127]
        masks = [[match[k][m] & keep[m] for m in range(4)] for k in range(4)]
        for t in range(16):
            v = adj[8 * t : 8 * t + 8, :]
            shifted = [pltpu.roll(v, 1, 0), pltpu.roll(v, 7, 0), pltpu.roll(v, 1, 1), pltpu.roll(v, 127, 1)]
            for k in range(4):
                value = zero
                for m in range(4):
                    value = jnp.where(masks[k][m], shifted[m], value)
                nb[k, 8 * t : 8 * t + 8, :] = value

    def gather_outer():
        match = matches()
        none = jnp.full((8, 128), 9.0, F32)
        along_x, along_y = none, none
        for k in range(4):
            along_x = jnp.where((even & match[k][0]) | (odd & match[k][1]), float(k), along_x)
            first, last = match[k][2] & (lane == 0), match[k][3] & (lane == 127)
            along_y = jnp.where(first | last, float(k), along_y)
        pick_x = jnp.concatenate([along_x] * 2, axis=0).astype(BF16)
        pick_y = jnp.concatenate([along_y] * 2, axis=0).astype(BF16)

        def body(i, carry):
            for t in range(8):
                rows = slice(16 * t, 16 * t + 16)
                a = [off[k, i, rows, :] for k in range(4)]
                for pick, out in ((pick_x, off_x), (pick_y, off_y)):
                    value = jnp.zeros((16, 128), BF16)
                    for k in range(4):
                        value = jnp.where(pick == BF16(k), a[k], value)
                    out[i, rows, :] = value
            return carry

        lax.fori_loop(0, 64, body, 0)

    def outer_x(n):
        for t in range(8):
            lo, hi = hxr[n, 0, 8 * t : 8 * t + 8, :], hxr[n, 1, 8 * t : 8 * t + 8, :]
            halo[8 * t : 8 * t + 8, :] = jnp.where(even, pltpu.roll(lo, 7, 0), pltpu.roll(hi, 1, 0))
            halo[64 + 8 * t : 72 + 8 * t, :] = jnp.where(even, lo, hi)

    def outer_y(n):
        below, above = hyr[n, 0], hyr[n, 1]
        for t in range(16):
            lo = pltpu.roll(below, 128 - t, 1) if t else below
            halo[8 * t : 8 * t + 8, :] = jnp.where(lane == 0, lo, pltpu.roll(above, 127 - t, 1))

    def routes(block, carry):
        far, oy = block // 8, block % 8
        to_core = core + far - 2 * core * far
        to_half = (half + lax.broadcasted_iota(jnp.int32, (8, 256), 0)) % 8
        rank = to_half * 16 + to_core * 8 + (iy + oy) % 8
        slot = jnp.full((8, 256), -1, jnp.int32)
        weight = jnp.zeros((8, 256), F32)
        for r in range(16):
            hit = odev[r : r + 1, :] == rank
            slot = jnp.where(hit, oslot[r : r + 1, :], slot)
            weight = jnp.where(hit, fw[r : r + 1, :], weight)
        route_send[far, oy, :8, :] = slot.astype(F32)
        route_send[far, oy, 8:, :] = weight
        return carry


    def route_copies(o):
        return [
            remote(route_send.at[0, o], route_near.at[o], rt_send.at[0, o], rt_recv.at[0, o], gy_peer(o)),
            remote(route_send.at[1, o], route_far.at[o], rt_send.at[1, o], rt_recv.at[1, o], gy_peer(o)),
        ]

    def start_residual(t, x):
        res[eight(t), :] = rhs[eight(t), :] - x

    def lower_residual(t, x):
        res[eight(t), :] = res[eight(t), :] - x

    def raise_adjoint(t, x):
        adj[eight(t), :] = adj[eight(t), :] + x

    def inner_off():
        matvec([(off.at[k], nb.at[k]) for k in range(4)], lower_residual, 4, 2)

    column = lax.broadcasted_iota(jnp.int32, (256, 256), 1).astype(F32).astype(BF16)

    def build(table, base):
        def body(s, carry):
            slots = jnp.transpose(table[s, :8, :]).astype(BF16)
            for d in range(8):
                hit = jnp.broadcast_to(slots[:, d : d + 1], (256, 256)) == column
                onehot[base + s, d] = jnp.where(hit, BF16(1), BF16(0))
            return carry

        lax.fori_loop(0, 8, body, 0)

    loads[0].wait()
    pack_x(0)
    pack_y(0)
    for n in (1, 2, 3):
        loads[n].wait()
    lax.fori_loop(0, 16, routes, 0)
    route_near[0] = route_send[0, 0]
    route_far[0] = route_send[1, 0]
    pl.semaphore_wait(barrier, 16)
    for copy in halo_copies(0):
        copy.start()
    for n in (4, 5, 6):
        loads[n].wait()
    matvec([(diag, adj)], start_residual, 8, 1)
    inner_neighbours()
    for k in range(4):
        loads[7 + k].wait()
    gather_outer()
    inner_off()
    loads[11].wait()
    loads[12].wait()
    loads[13].wait()
    d = dens[...]
    factor[...] = -3.0 * d * d * d * fu[...]
    for b in range(2):
        dens2[:, 128 * b : 128 * b + 128] = dens[pl.ds(b, 64, 2), :]

    for n in range(SWEEPS):
        copies = halo_copies(n)
        if n:
            pack_x(n)
            copies[0].start()
            copies[1].start()
            pack_y(n)
            copies[2].start()
            copies[3].start()
            matvec([(diag, adj)], start_residual, 8, 1)
            inner_neighbours()
            inner_off()
        copies[2].wait_recv()
        copies[3].wait_recv()
        outer_y(n)
        matvec([(off_y, halo)], lower_residual, 8, 1)
        copies[0].wait_recv()
        copies[1].wait_recv()
        if n == 0:
            for o in range(1, 8):
                for copy in route_copies(o):
                    copy.start()
        outer_x(n)
        matvec([(off_x, halo)], lower_residual, 8, 2)
        matvec([(smooth, res)], raise_adjoint, 8, 2)

    adj_copy = pltpu.make_async_copy(adj, adj_out, out_sem.at[0])
    adj_copy.start()
    own[...] = factor[...] * adj[...]
    for b in range(2):
        xg[0, :, 128 * b : 128 * b + 128] = own[pl.ds(b, 64, 2), :]

    spread = {
        o: remote(xg.at[0], xg.at[o], xg_send.at[o], xg_recv.at[o], gy_peer(o)) for o in range(1, 8)
    }
    for o in (4, 3, 5, 1, 7, 2, 6):
        spread[o].start()
    for o in range(1, 8):
        for copy in route_copies(o):
            copy.wait_recv()
    build(route_far, 8)
    build(route_near, 0)

    def partial(far, d):
        table = route_far if far else route_near
        out = jnp.zeros((144, 256), F32)
        for o in range(8):
            w = table[o, pl.ds(8 + d, 1), :]
            p = xg[o] * w
            top = p.astype(BF16)
            rest = (p - top.astype(F32)).astype(BF16)
            w16 = jnp.broadcast_to(w, (16, 256))
            wtop = w16.astype(BF16).astype(F32)
            r16 = lax.broadcasted_iota(jnp.int32, (16, 256), 0)
            tail = jnp.where(r16 == 0, wtop, jnp.where(r16 == 1, w16 - wtop, 0.0)).astype(BF16)
            lhs = jnp.concatenate([top, rest, tail], axis=0)
            out += lax.dot_general(lhs, onehot[8 * far + o, d], NN, preferred_element_type=F32)
        return out[:64] + out[64:128], out[128:136] + pltpu.roll(out[128:136], 7, 0)

    def cross_copy(d):
        return remote(cs.at[d], cr.at[d], xc_send.at[d], xc_recv.at[d], (partner, iy))

    def reduce_copy(d):
        return remote(ps.at[d], pr.at[d], rs_send.at[d], rs_recv.at[d], gx_peer(d))

    def turn(k):
        return (2 * k + 3 - 9 * (k // 4)) % 8

    def send_cross(d):
        values, weights = partial(1, d)
        cs[d, :64] = values
        cs[d, 64:] = weights
        cross_copy(d).start()

    def send_partial(k, carry, ahead):
        d = turn(k)

        if ahead:
            send_cross(turn(k + AHEAD))
        values, weights = partial(0, d)
        cross_copy(d).wait_recv()
        ps[d, :64] = values + cr[d, :64]
        ps[d, 64:] = weights + cr[d, 64:]
        reduce_copy(d).start()
        return carry

    for o in (2, 6, 1, 7, 4, 3, 5):
        spread[o].wait_recv()
    for k in range(AHEAD):
        send_cross(turn(k))
    lax.fori_loop(0, 8 - AHEAD, functools.partial(send_partial, ahead=True), 0, unroll=2)
    lax.fori_loop(8 - AHEAD, 7, functools.partial(send_partial, ahead=False), 0)
    values, weights = partial(0, 0)
    cross_copy(0).wait_recv()
    values += cr[0, :64]
    weights += cr[0, 64:]
    for d in (2, 4, 6, 7, 1, 3, 5):
        reduce_copy(d).wait_recv()
        values += pr[d, :64]
        weights += pr[d, 64:]
    total = weights[0:1]
    result = (xg[0] + values) / (dens2[...] * (1.0 + total))
    for b in range(2):
        filt[pl.ds(b, 64, 2), :] = result[:, 128 * b : 128 * b + 128]
    filt_copy = pltpu.make_async_copy(filt, filt_out, out_sem.at[1])
    filt_copy.start()

    for n in range(SWEEPS):
        for copy in halo_copies(n):
            copy.wait_send()
    for o in range(1, 8):
        for copy in route_copies(o):
            copy.wait_send()
        spread[o].wait_send()
        reduce_copy(o).wait_send()
    for d in range(8):
        cross_copy(d).wait_send()
    adj_copy.wait()
    filt_copy.wait()


def hand_over(a, b, a_out, b_out):
    a_out[...] = a[...]
    b_out[...] = b[...]


def local(lam_start, adj_rhs, a_diag, a_off, cols, smoother, forward_u, density, owner_dev, owner_slot, filt_weight):
    width, rows_x, rows_y = lam_start.shape
    rows = width * rows_x

    def by_row(x):
        return x.reshape(x.shape[:-3] + (rows, rows_y))

    def by_owner(x):
        return jnp.transpose(x, (0, 1, 3, 2)).reshape(x.shape[3], x.shape[2])

    any_spec = pl.BlockSpec(memory_space=pl.ANY)
    dma = pltpu.SemaphoreType.DMA
    vm = pltpu.VMEM
    adjoint, filtered = pl.pallas_call(
        kernel,
        out_shape=[jax.ShapeDtypeStruct((rows, rows_y), F32)] * 2,
        in_specs=[any_spec] * 11,
        out_specs=[any_spec] * 2,
        scratch_shapes=[
            vm((128, 128), F32), vm((128, 128), F32), vm((64, 128, 128), BF16), vm((4, 64, 128, 128), BF16),
            vm((64, 128, 128), BF16), vm((4, 2, 128), jnp.int32), vm((128, 128), F32), vm((128, 128), F32),
            vm((16, 256), jnp.int32), vm((16, 256), jnp.int32), vm((16, 256), F32),
            vm((128, 128), F32), vm((4, 128, 128), F32), vm((64, 128, 128), BF16), vm((64, 128, 128), BF16),
            vm((128, 128), F32), vm((3, 2, 64, 128), F32), vm((3, 2, 64, 128), F32),
            vm((3, 2, 8, 128), F32), vm((3, 2, 8, 128), F32), vm((128, 128), F32),
            vm((2, 8, 16, 256), F32), vm((8, 16, 256), F32), vm((8, 16, 256), F32),
            vm((16, 8, 256, 256), BF16), vm((8, 64, 256), F32), vm((64, 256), F32), vm((128, 128), F32),
            vm((8, 72, 256), F32), vm((8, 72, 256), F32),
            vm((8, 72, 256), F32), vm((8, 72, 256), F32), vm((128, 128), F32),
            dma((14,)), dma((2,)), dma((3, 2)), dma((3, 2)), dma((3, 2)), dma((3, 2)), dma((2, 8)), dma((2, 8)),
            dma((8,)), dma((8,)), dma((8,)), dma((8,)), dma((8,)), dma((8,)),
        ],
        compiler_params=pltpu.CompilerParams(
            collective_id=0, has_side_effects=True, vmem_limit_bytes=56 * 2**20
        ),
        name="sweeps_and_filter",
    )(
        by_row(lam_start), by_row(adj_rhs), by_row(a_diag), by_row(a_off), cols, by_row(smoother),
        by_row(forward_u), by_row(density), by_owner(owner_dev), by_owner(owner_slot), by_owner(filt_weight),
    )
    adjoint, filtered = pl.pallas_call(
        hand_over,
        out_shape=[jax.ShapeDtypeStruct((rows, rows_y), F32)] * 2,
        in_specs=[pl.BlockSpec(memory_space=vm)] * 2,
        out_specs=[pl.BlockSpec(memory_space=vm)] * 2,
        name="hand_over",
    )(adjoint, filtered)
    shape = (width, rows_x, rows_y)
    return adjoint.reshape(shape), filtered.reshape(shape)


def solution(mesh):
    in_specs = (
        P(None, "gx", "gy"),
        P(None, "gx", "gy"),
        P(None, None, "gx", "gy"),
        P(None, None, None, "gx", "gy"),
        P(None, "gx", "gy"),
        P(None, None, "gx", "gy"),
        P(None, "gx", "gy"),
        P(None, "gx", "gy"),
        P("gx", "gy", None, None),
        P("gx", "gy", None, None),
        P("gx", "gy", None, None),
    )
    out_specs = (P(None, "gx", "gy"), P(None, "gx", "gy"))
    return jax.shard_map(local, mesh=mesh, in_specs=in_specs, out_specs=out_specs, check_vma=False)
```

```python
import functools

import jax
import jax.numpy as jnp
from jax import lax
from jax.experimental import pallas as pl
from jax.experimental.pallas import tpu as pltpu
from jax.sharding import PartitionSpec as P

SWEEPS = 3
F32 = jnp.float32
BF16 = jnp.bfloat16
MESH = pl.DeviceIdType.MESH
NN = (((1,), (0,)), ((), ()))
AHEAD = 2


def merge4(accs, row):
    def step(p, q, mask, shift):
        return jnp.where(mask, p, q) + pltpu.roll(jnp.where(mask, q, p), shift, 0)

    low = (row % 4) < 2
    first = step(accs[0], accs[1], low, 6)
    second = step(accs[2], accs[3], low, 6)
    return step(first, second, row < 4, 4)


def matvec(pairs, write, group, unroll):
    row = lax.broadcasted_iota(jnp.int32, (8, 128), 0)

    def body(g, carry):
        accs = [None] * group
        for blocks, vector in pairs:
            for t in range(8):
                v = vector[16 * t : 16 * t + 16, :]
                for q in range(group):
                    p = blocks[g * group + q, 16 * t : 16 * t + 16, :].astype(F32) * v
                    accs[q] = p[:8] + p[8:] if accs[q] is None else (accs[q] + p[:8]) + p[8:]
        for h in range(group // 4):
            write(g * (group // 4) + h, merge4(accs[4 * h : 4 * h + 4], row))
        return carry

    lax.fori_loop(0, 64 // group, body, 0, unroll=unroll)


def eight(t):
    return pl.ds(pl.multiple_of(t * 8, 8), 8)


def kernel(
    lam_hbm, rhs_hbm, diag_hbm, off_hbm, cols_hbm, smooth_hbm, fu_hbm, dens_hbm, odev_hbm, oslot_hbm, fw_hbm,
    adj_out, filt_out,
    adj, rhs, diag, off, smooth, cols, fu, dens, odev, oslot, fw,
    res, nb, off_x, off_y, halo, hxs, hxr, hys, hyr, own, route_send, route_near, route_far, onehot, xg, dens2, factor, cs, cr, ps, pr, filt,
    in_sem, out_sem, hx_send, hx_recv, hy_send, hy_recv, rt_send, rt_recv, xg_send, xg_recv, xc_send, xc_recv,
    rs_send, rs_recv,
):
    ix = lax.axis_index("gx")
    iy = lax.axis_index("gy")
    half = ix // 2
    core = ix % 2
    partner = half * 2 + 1 - core

    def gy_peer(o):
        return (ix, lax.rem(iy + o, 8))

    def gx_peer(o):
        return (lax.rem(half + o, 8) * 2 + core, iy)

    right = lax.rem(ix + 1, 16)
    left = lax.rem(ix + 15, 16)

    sources = [
        (lam_hbm, adj), (odev_hbm, odev), (oslot_hbm, oslot), (fw_hbm, fw), (cols_hbm, cols), (rhs_hbm, rhs),
        (diag_hbm, diag), (off_hbm.at[0], off.at[0]), (off_hbm.at[1], off.at[1]), (off_hbm.at[2], off.at[2]),
        (off_hbm.at[3], off.at[3]), (smooth_hbm, smooth), (fu_hbm, fu), (dens_hbm, dens),
    ]
    loads = [pltpu.make_async_copy(a, b, in_sem.at[n]) for n, (a, b) in enumerate(sources)]
    for load in loads:
        load.start()

    barrier = pltpu.get_barrier_semaphore()
    for o in range(1, 8):
        pl.semaphore_signal(barrier, inc=1, device_id=gy_peer(o), device_id_type=MESH)
        pl.semaphore_signal(barrier, inc=1, device_id=gx_peer(o), device_id_type=MESH)
    for x in (right, left):
        pl.semaphore_signal(barrier, inc=1, device_id=(x, iy), device_id_type=MESH)

    row = lax.broadcasted_iota(jnp.int32, (8, 128), 0)
    lane = lax.broadcasted_iota(jnp.int32, (8, 128), 1)
    odd = (row % 2) == 1
    even = (row % 2) == 0

    def remote(src, dst, send, recv, device):
        return pltpu.make_async_remote_copy(
            src_ref=src, dst_ref=dst, send_sem=send, recv_sem=recv, device_id=device, device_id_type=MESH
        )

    def halo_copies(n):
        return [
            remote(hxs.at[n, 0], hxr.at[n, 0], hx_send.at[n, 0], hx_recv.at[n, 0], (right, iy)),
            remote(hxs.at[n, 1], hxr.at[n, 1], hx_send.at[n, 1], hx_recv.at[n, 1], (left, iy)),
            remote(hys.at[n, 0], hyr.at[n, 0], hy_send.at[n, 0], hy_recv.at[n, 0], gy_peer(1)),
            remote(hys.at[n, 1], hyr.at[n, 1], hy_send.at[n, 1], hy_recv.at[n, 1], gy_peer(7)),
        ]

    def pack_x(n):
        for t in range(8):
            v, w = adj[8 * t : 8 * t + 8, :], adj[64 + 8 * t : 72 + 8 * t, :]
            hxs[n, 0, 8 * t : 8 * t + 8, :] = jnp.where(odd, v, pltpu.roll(w, 7, 0))
            hxs[n, 1, 8 * t : 8 * t + 8, :] = jnp.where(even, v, pltpu.roll(w, 1, 0))

    def pack_y(n):
        up = jnp.zeros((8, 128), F32)
        down = jnp.zeros((8, 128), F32)
        for t in range(16):
            v = adj[8 * t : 8 * t + 8, :]
            up = jnp.where(lane == t, pltpu.roll(v, t + 1, 1), up)
            down = jnp.where(lane == t, pltpu.roll(v, t, 1) if t else v, down)
        hys[n, 0] = up
        hys[n, 1] = down

    def matches():
        x = ix * 2 + row % 2
        y = iy * 128 + lane
        here = x * 1024 + y
        expects = [
            jnp.where(x >= 1, here - 1024, -5),
            jnp.where(x < 31, here + 1024, -5),
            jnp.where(y >= 1, here - 1, -5),
            jnp.where(y < 1023, here + 1, -5),
        ]
        named = [jnp.concatenate([cols[k]] * 4, axis=0) for k in range(4)]
        return [[named[k] == e for e in expects] for k in range(4)]

    def inner_neighbours():
        match = matches()
        zero = jnp.zeros((8, 128), F32)
        keep = [odd, even, lane > 0, lane < 127]
        masks = [[match[k][m] & keep[m] for m in range(4)] for k in range(4)]
        for t in range(16):
            v = adj[8 * t : 8 * t + 8, :]
            shifted = [pltpu.roll(v, 1, 0), pltpu.roll(v, 7, 0), pltpu.roll(v, 1, 1), pltpu.roll(v, 127, 1)]
            for k in range(4):
                value = zero
                for m in range(4):
                    value = jnp.where(masks[k][m], shifted[m], value)
                nb[k, 8 * t : 8 * t + 8, :] = value

    def gather_outer():
        match = matches()
        none = jnp.full((8, 128), 9.0, F32)
        along_x, along_y = none, none
        for k in range(4):
            along_x = jnp.where((even & match[k][0]) | (odd & match[k][1]), float(k), along_x)
            first, last = match[k][2] & (lane == 0), match[k][3] & (lane == 127)
            along_y = jnp.where(first | last, float(k), along_y)
        pick_x = jnp.concatenate([along_x] * 2, axis=0).astype(BF16)
        pick_y = jnp.concatenate([along_y] * 2, axis=0).astype(BF16)

        def body(i, carry):
            for t in range(8):
                rows = slice(16 * t, 16 * t + 16)
                a = [off[k, i, rows, :] for k in range(4)]
                for pick, out in ((pick_x, off_x), (pick_y, off_y)):
                    value = jnp.zeros((16, 128), BF16)
                    for k in range(4):
                        value = jnp.where(pick == BF16(k), a[k], value)
                    out[i, rows, :] = value
            return carry

        lax.fori_loop(0, 64, body, 0)

    def outer_x(n):
        for t in range(8):
            lo, hi = hxr[n, 0, 8 * t : 8 * t + 8, :], hxr[n, 1, 8 * t : 8 * t + 8, :]
            halo[8 * t : 8 * t + 8, :] = jnp.where(even, pltpu.roll(lo, 7, 0), pltpu.roll(hi, 1, 0))
            halo[64 + 8 * t : 72 + 8 * t, :] = jnp.where(even, lo, hi)

    def outer_y(n):
        below, above = hyr[n, 0], hyr[n, 1]
        for t in range(16):
            lo = pltpu.roll(below, 128 - t, 1) if t else below
            halo[8 * t : 8 * t + 8, :] = jnp.where(lane == 0, lo, pltpu.roll(above, 127 - t, 1))

    def routes(block, carry):
        far, oy = block // 8, block % 8
        to_core = core + far - 2 * core * far
        to_half = (half + lax.broadcasted_iota(jnp.int32, (8, 256), 0)) % 8
        rank = to_half * 16 + to_core * 8 + (iy + oy) % 8
        slot = jnp.full((8, 256), -1, jnp.int32)
        weight = jnp.zeros((8, 256), F32)
        for r in range(16):
            hit = odev[r : r + 1, :] == rank
            slot = jnp.where(hit, oslot[r : r + 1, :], slot)
            weight = jnp.where(hit, fw[r : r + 1, :], weight)
        route_send[far, oy, :8, :] = slot.astype(F32)
        route_send[far, oy, 8:, :] = weight
        return carry


    def route_copies(o):
        return [
            remote(route_send.at[0, o], route_near.at[o], rt_send.at[0, o], rt_recv.at[0, o], gy_peer(o)),
            remote(route_send.at[1, o], route_far.at[o], rt_send.at[1, o], rt_recv.at[1, o], gy_peer(o)),
        ]

    def start_residual(t, x):
        res[eight(t), :] = rhs[eight(t), :] - x

    def lower_residual(t, x):
        res[eight(t), :] = res[eight(t), :] - x

    def raise_adjoint(t, x):
        adj[eight(t), :] = adj[eight(t), :] + x

    def inner_off():
        matvec([(off.at[k], nb.at[k]) for k in range(4)], lower_residual, 4, 2)

    column = lax.broadcasted_iota(jnp.int32, (256, 256), 1).astype(F32).astype(BF16)

    def build(table, base):
        def body(s, carry):
            slots = jnp.transpose(table[s, :8, :]).astype(BF16)
            for d in range(8):
                hit = jnp.broadcast_to(slots[:, d : d + 1], (256, 256)) == column
                onehot[base + s, d] = jnp.where(hit, BF16(1), BF16(0))
            return carry

        lax.fori_loop(0, 8, body, 0)

    loads[0].wait()
    pack_x(0)
    pack_y(0)
    for n in (1, 2, 3):
        loads[n].wait()
    lax.fori_loop(0, 16, routes, 0)
    route_near[0] = route_send[0, 0]
    route_far[0] = route_send[1, 0]
    pl.semaphore_wait(barrier, 16)
    for copy in halo_copies(0):
        copy.start()
    for n in (4, 5, 6):
        loads[n].wait()
    matvec([(diag, adj)], start_residual, 8, 1)
    inner_neighbours()
    for k in range(4):
        loads[7 + k].wait()
    gather_outer()
    inner_off()
    loads[11].wait()
    loads[12].wait()
    loads[13].wait()
    d = dens[...]
    factor[...] = -3.0 * d * d * d * fu[...]
    for b in range(2):
        dens2[:, 128 * b : 128 * b + 128] = dens[pl.ds(b, 64, 2), :]

    for n in range(SWEEPS):
        copies = halo_copies(n)
        if n:
            pack_x(n)
            copies[0].start()
            copies[1].start()
            pack_y(n)
            copies[2].start()
            copies[3].start()
            matvec([(diag, adj)], start_residual, 8, 1)
            inner_neighbours()
            inner_off()
        copies[2].wait_recv()
        copies[3].wait_recv()
        outer_y(n)
        matvec([(off_y, halo)], lower_residual, 8, 1)
        copies[0].wait_recv()
        copies[1].wait_recv()
        if n == 0:
            for o in range(1, 8):
                for copy in route_copies(o):
                    copy.start()
        outer_x(n)
        matvec([(off_x, halo)], lower_residual, 8, 2)
        matvec([(smooth, res)], raise_adjoint, 8, 2)

    adj_copy = pltpu.make_async_copy(adj, adj_out, out_sem.at[0])
    adj_copy.start()
    own[...] = factor[...] * adj[...]
    for b in range(2):
        xg[0, :, 128 * b : 128 * b + 128] = own[pl.ds(b, 64, 2), :]

    spread = {
        o: remote(xg.at[0], xg.at[o], xg_send.at[o], xg_recv.at[o], gy_peer(o)) for o in range(1, 8)
    }
    for o in (3, 5, 1, 7, 4, 2, 6):
        spread[o].start()
    for o in range(1, 8):
        for copy in route_copies(o):
            copy.wait_recv()
    build(route_far, 8)
    build(route_near, 0)

    def partial(far, d):
        table = route_far if far else route_near
        out = jnp.zeros((144, 256), F32)
        for o in range(8):
            w = table[o, pl.ds(8 + d, 1), :]
            p = xg[o] * w
            top = p.astype(BF16)
            rest = (p - top.astype(F32)).astype(BF16)
            w16 = jnp.broadcast_to(w, (16, 256))
            wtop = w16.astype(BF16).astype(F32)
            r16 = lax.broadcasted_iota(jnp.int32, (16, 256), 0)
            tail = jnp.where(r16 == 0, wtop, jnp.where(r16 == 1, w16 - wtop, 0.0)).astype(BF16)
            lhs = jnp.concatenate([top, rest, tail], axis=0)
            out += lax.dot_general(lhs, onehot[8 * far + o, d], NN, preferred_element_type=F32)
        return out[:64] + out[64:128], out[128:136] + pltpu.roll(out[128:136], 7, 0)

    def cross_copy(d):
        return remote(cs.at[d], cr.at[d], xc_send.at[d], xc_recv.at[d], (partner, iy))

    def reduce_copy(d):
        return remote(ps.at[d], pr.at[d], rs_send.at[d], rs_recv.at[d], gx_peer(d))

    def turn(k):
        return (2 * k + 3 - 9 * (k // 4)) % 8

    def send_cross(d):
        values, weights = partial(1, d)
        cs[d, :64] = values
        cs[d, 64:] = weights
        cross_copy(d).start()

    def send_partial(k, carry, ahead):
        d = turn(k)

        if ahead:
            send_cross(turn(k + AHEAD))
        values, weights = partial(0, d)
        cross_copy(d).wait_recv()
        ps[d, :64] = values + cr[d, :64]
        ps[d, 64:] = weights + cr[d, 64:]
        reduce_copy(d).start()
        return carry

    for o in (2, 6, 1, 7, 4, 3, 5):
        spread[o].wait_recv()
    for k in range(AHEAD):
        send_cross(turn(k))
    lax.fori_loop(0, 8 - AHEAD, functools.partial(send_partial, ahead=True), 0, unroll=2)
    lax.fori_loop(8 - AHEAD, 7, functools.partial(send_partial, ahead=False), 0)
    values, weights = partial(0, 0)
    cross_copy(0).wait_recv()
    values += cr[0, :64]
    weights += cr[0, 64:]
    for d in (2, 4, 6, 7, 1, 3, 5):
        reduce_copy(d).wait_recv()
        values += pr[d, :64]
        weights += pr[d, 64:]
    total = weights[0:1]
    result = (xg[0] + values) / (dens2[...] * (1.0 + total))
    for b in range(2):
        filt[pl.ds(b, 64, 2), :] = result[:, 128 * b : 128 * b + 128]
    filt_copy = pltpu.make_async_copy(filt, filt_out, out_sem.at[1])
    filt_copy.start()

    for n in range(SWEEPS):
        for copy in halo_copies(n):
            copy.wait_send()
    for o in range(1, 8):
        for copy in route_copies(o):
            copy.wait_send()
        spread[o].wait_send()
        reduce_copy(o).wait_send()
    for d in range(8):
        cross_copy(d).wait_send()
    adj_copy.wait()
    filt_copy.wait()


def hand_over(a, b, a_out, b_out):
    a_out[...] = a[...]
    b_out[...] = b[...]


def local(lam_start, adj_rhs, a_diag, a_off, cols, smoother, forward_u, density, owner_dev, owner_slot, filt_weight):
    width, rows_x, rows_y = lam_start.shape
    rows = width * rows_x

    def by_row(x):
        return x.reshape(x.shape[:-3] + (rows, rows_y))

    def by_owner(x):
        return jnp.transpose(x, (0, 1, 3, 2)).reshape(x.shape[3], x.shape[2])

    any_spec = pl.BlockSpec(memory_space=pl.ANY)
    dma = pltpu.SemaphoreType.DMA
    vm = pltpu.VMEM
    adjoint, filtered = pl.pallas_call(
        kernel,
        out_shape=[jax.ShapeDtypeStruct((rows, rows_y), F32)] * 2,
        in_specs=[any_spec] * 11,
        out_specs=[any_spec] * 2,
        scratch_shapes=[
            vm((128, 128), F32), vm((128, 128), F32), vm((64, 128, 128), BF16), vm((4, 64, 128, 128), BF16),
            vm((64, 128, 128), BF16), vm((4, 2, 128), jnp.int32), vm((128, 128), F32), vm((128, 128), F32),
            vm((16, 256), jnp.int32), vm((16, 256), jnp.int32), vm((16, 256), F32),
            vm((128, 128), F32), vm((4, 128, 128), F32), vm((64, 128, 128), BF16), vm((64, 128, 128), BF16),
            vm((128, 128), F32), vm((3, 2, 64, 128), F32), vm((3, 2, 64, 128), F32),
            vm((3, 2, 8, 128), F32), vm((3, 2, 8, 128), F32), vm((128, 128), F32),
            vm((2, 8, 16, 256), F32), vm((8, 16, 256), F32), vm((8, 16, 256), F32),
            vm((16, 8, 256, 256), BF16), vm((8, 64, 256), F32), vm((64, 256), F32), vm((128, 128), F32),
            vm((8, 72, 256), F32), vm((8, 72, 256), F32),
            vm((8, 72, 256), F32), vm((8, 72, 256), F32), vm((128, 128), F32),
            dma((14,)), dma((2,)), dma((3, 2)), dma((3, 2)), dma((3, 2)), dma((3, 2)), dma((2, 8)), dma((2, 8)),
            dma((8,)), dma((8,)), dma((8,)), dma((8,)), dma((8,)), dma((8,)),
        ],
        compiler_params=pltpu.CompilerParams(
            collective_id=0, has_side_effects=True, vmem_limit_bytes=56 * 2**20
        ),
        name="sweeps_and_filter",
    )(
        by_row(lam_start), by_row(adj_rhs), by_row(a_diag), by_row(a_off), cols, by_row(smoother),
        by_row(forward_u), by_row(density), by_owner(owner_dev), by_owner(owner_slot), by_owner(filt_weight),
    )
    adjoint, filtered = pl.pallas_call(
        hand_over,
        out_shape=[jax.ShapeDtypeStruct((rows, rows_y), F32)] * 2,
        in_specs=[pl.BlockSpec(memory_space=vm)] * 2,
        out_specs=[pl.BlockSpec(memory_space=vm)] * 2,
        name="hand_over",
    )(adjoint, filtered)
    shape = (width, rows_x, rows_y)
    return adjoint.reshape(shape), filtered.reshape(shape)


def solution(mesh):
    in_specs = (
        P(None, "gx", "gy"),
        P(None, "gx", "gy"),
        P(None, None, "gx", "gy"),
        P(None, None, None, "gx", "gy"),
        P(None, "gx", "gy"),
        P(None, None, "gx", "gy"),
        P(None, "gx", "gy"),
        P(None, "gx", "gy"),
        P("gx", "gy", None, None),
        P("gx", "gy", None, None),
        P("gx", "gy", None, None),
    )
    out_specs = (P(None, "gx", "gy"), P(None, "gx", "gy"))
    return jax.shard_map(local, mesh=mesh, in_specs=in_specs, out_specs=out_specs, check_vma=False)
```
